128 devices in a mesh: fa: 8 (over z, core), fb: 16 (over x, y).
Axes of the slice: x: 4, y: 4, z: 4, core: 2. Of those that a mesh axis runs over, the one named last changes fastest.
Arguments:
- queries: bfloat16 [128, 256, 2560], P(('fa', 'fb')), may hold values from -8 to 8
- keys: bfloat16 [128, 256, 2560], P(('fa', 'fb')), may hold values from -8 to 8
- values: bfloat16 [128, 256, 2560], P(('fa', 'fb')), may hold values from -6 to 6
- lengths: int32 [128], P(('fa', 'fb')), may hold values from 64 to 256, as said below
- head_kind: int32 [20], replicated, may hold values from 0 to 1, as said below
Outputs:
- attended: bfloat16 [128, 256, 2560], P(('fa', 'fb'))
The draws below stay inside these ranges and needn't reach their ends.
Inputs may be any that keep to these rules, and one draw needn't show every extreme that they name: `lengths`: every frame's live positions are a prefix; some frame has all 256 live. `head_kind`: at least one head of each kind.
All inputs are finite; a program needn't handle non-finite values.
Results may differ from the reference program's by a relative error of at most 0.0044.
Values may be sent and summed in bfloat16 or wider, within the bound.
No kernel may reach another device: no remote copies, remote signals or barrier semaphores. Data moves between devices by JAX's collectives and lax.ppermute only.
A program may use at most 64 MiB of HBM per device.

```python
import jax
import jax.numpy as jnp
from jax import lax

HEADS = 20
HEAD_DIM = 128
WIDTH = 2560
POS = 256
FRAMES = 128


def draw_queries(key, part):
    key = jax.random.fold_in(key, 11)
    drawn = jnp.clip(jax.random.normal(key, (FRAMES, POS, WIDTH), jnp.float32), -6.0, 6.0)
    return drawn.astype(jnp.bfloat16)


def draw_keys(key, part):
    key = jax.random.fold_in(key, 23)
    drawn = jnp.clip(jax.random.normal(key, (FRAMES, POS, WIDTH), jnp.float32), -6.0, 6.0)
    return drawn.astype(jnp.bfloat16)


def draw_lengths(key, part):
    key = jax.random.fold_in(key, 37)
    drawn = jax.random.randint(key, (FRAMES,), POS // 4, POS + 1, jnp.int32)
    return drawn.at[0].set(POS)


def draw_head_kind(key, part):
    key = jax.random.fold_in(key, 41)
    first, second = jax.random.split(key)
    spatial_count = jax.random.randint(first, (), 1, HEADS, jnp.int32)
    order = jax.random.permutation(second, HEADS)
    return (order < spatial_count).astype(jnp.int32)


def block_scale(rng, dims, pieces, least, high):
    def one(axis_at, shards_of):
        heights = jax.random.uniform(jax.random.fold_in(jax.random.fold_in(rng, 6), axis_at), (shards_of,), jnp.float32, least / len(pieces), high / len(pieces))
        return jnp.repeat(jnp.exp(heights), dims[axis_at] // shards_of).reshape((-1,) + (1,) * (len(dims) - axis_at - 1))

    factor_of = one(*pieces[0])
    for cut in pieces[1:]:
        factor_of = factor_of * one(*cut)
    return factor_of


def gaussian(key, dims, deviation, most, pieces=(), held_as=jnp.bfloat16):
    factor_of = block_scale(key, dims, pieces, -0.22, 0.18) if pieces else 1.0
    array = jax.random.normal(key, dims, jnp.float32) * deviation * factor_of
    return jnp.minimum(jnp.maximum(array, -most), most).astype(held_as)


def setup_inputs(seed: int = 0) -> dict:
    seeds = jax.random.split(jax.random.key(seed), 6)
    return {
        "queries": draw_queries(jax.random.fold_in(seeds[5], 71), 0),
        "keys": draw_keys(jax.random.fold_in(seeds[5], 71), 0),
        "values": gaussian(seeds[2], (FRAMES, POS, WIDTH), 1.0, 6.0, ((0, 128),)),
        "lengths": draw_lengths(jax.random.fold_in(seeds[5], 71), 0),
        "head_kind": draw_head_kind(jax.random.fold_in(seeds[5], 71), 0),
    }


def spatial_frame(query_frame, key_frame, value_frame, frame_length):
    score_scale = 1.0 / jnp.sqrt(jnp.float32(HEAD_DIM))
    query_heads = query_frame.reshape(POS, HEADS, HEAD_DIM).transpose(1, 0, 2).astype(jnp.float32)
    key_heads = key_frame.reshape(POS, HEADS, HEAD_DIM).transpose(1, 0, 2).astype(jnp.float32)
    value_heads = value_frame.reshape(POS, HEADS, HEAD_DIM).transpose(1, 0, 2).astype(jnp.float32)
    scores = jnp.einsum('hpd,hqd->hpq', query_heads, key_heads) * score_scale
    valid_keys = jnp.arange(POS, dtype=jnp.int32) < frame_length
    scores = jnp.where(valid_keys[None, None, :], scores, jnp.float32(-1e+30))
    weights = jnp.exp(scores - lax.optimization_barrier(jnp.max(scores, axis=-1, keepdims=True)))
    totals = lax.optimization_barrier(jnp.sum(weights, axis=-1, keepdims=True))
    rounded = weights.astype(jnp.bfloat16).astype(jnp.float32)
    numer = jnp.einsum('hpq,hqd->hpd', rounded, value_heads)
    result = (numer / totals).astype(jnp.bfloat16)
    return result.transpose(1, 0, 2)

def temporal_block(block_args):
    query_block, key_block, value_block = block_args
    score_scale = 1.0 / jnp.sqrt(jnp.float32(HEAD_DIM))
    scores = jnp.einsum('fphd,gphd->phfg', query_block.astype(jnp.float32), key_block.astype(jnp.float32)) * score_scale
    weights = jnp.exp(scores - lax.optimization_barrier(jnp.max(scores, axis=-1, keepdims=True)))
    totals = lax.optimization_barrier(jnp.sum(weights, axis=-1))
    rounded = weights.astype(jnp.bfloat16).astype(jnp.float32)
    numer = jnp.einsum('phfg,gphd->fphd', rounded, value_block.astype(jnp.float32))
    return (numer / totals.transpose(2, 0, 1)[..., None]).astype(jnp.bfloat16)

def reference(queries, keys, values, lengths, head_kind):
    spatial = lax.map(lambda frame_args: spatial_frame(*frame_args), (queries, keys, values, lengths))
    block_rows = min(64, POS)
    block_count = POS // block_rows

    def split_blocks(whole):
        return whole.reshape(FRAMES, block_count, block_rows, HEADS, HEAD_DIM).transpose(1, 0, 2, 3, 4)
    temporal = lax.map(temporal_block, (split_blocks(queries), split_blocks(keys), split_blocks(values)))
    temporal = temporal.transpose(1, 0, 2, 3, 4).reshape(FRAMES, POS, HEADS, HEAD_DIM)
    chosen = jnp.where(head_kind[None, None, :, None] == 1, spatial, temporal)
    return chosen.reshape(FRAMES, POS, WIDTH)
```

```python
import functools

import jax
import jax.numpy as jnp
from jax import lax
from jax.experimental import pallas as pl
from jax.experimental.pallas import tpu as pltpu
from jax.sharding import PartitionSpec as P

HEADS = 20
HEAD_DIM = 128
SCALE = HEAD_DIM**-0.5
AXES = ("fa", "fb")
VMEM_LIMIT = 56 * 1024 * 1024


def list_heads(kind_ref, list_ref, wanted):
    def step(head, count):
        list_ref[count] = head
        return count + (kind_ref[head] == wanted).astype(jnp.int32)

    lax.fori_loop(0, HEADS, step, jnp.int32(0))


def head_columns(list_ref, place):
    return pl.ds(pl.multiple_of(list_ref[place] * HEAD_DIM, HEAD_DIM), HEAD_DIM)


def pack_kernel(
    count, devices, kind_ref, q_ref, k_ref, v_ref, out_ref, list_ref, held, wide, sems
):
    list_heads(kind_ref, list_ref, 0)
    rows = 6 * count
    sources = (q_ref, k_ref, v_ref)

    def fetch(which, place):
        return pltpu.make_async_copy(
            sources[which].at[:, head_columns(list_ref, place)],
            held.at[which * count + place],
            sems.at[which * count + place],
        )

    for place in range(count):
        for which in range(3):
            fetch(which, place).start()
    for place in range(count):
        for which in range(3):
            fetch(which, place).wait()
            slot = which * count + place
            for half in range(2):
                wide[pl.ds(2 * slot + half, devices, stride=rows), :] = held[
                    slot, half * devices : (half + 1) * devices, :
                ].astype(jnp.float32)
    step_rows = 16 * rows

    def narrow(step, carry):
        at = pl.ds(pl.multiple_of(step * step_rows, step_rows), step_rows)
        out_ref[at, :] = wide[at, :].astype(jnp.bfloat16)
        return carry

    lax.fori_loop(0, devices // 16, narrow, 0)


def attend(query, key, value, live):
    scores = lax.dot_general(
        query, key, (((1,), (1,)), ((), ())), preferred_element_type=jnp.float32
    )
    scores = scores * SCALE
    if live is not None:
        scores = jnp.where(live, scores, -1e30)
    weights = jnp.exp(scores - jnp.max(scores, axis=-1, keepdims=True))
    totals = jnp.sum(weights, axis=-1, keepdims=True)
    numer = jnp.dot(weights.astype(jnp.bfloat16), value, preferred_element_type=jnp.float32)
    return numer / totals


def temporal_kernel(count, devices, in_ref, out_ref, wide, result):
    rows = 6 * count
    back = 2 * count
    step_rows = 16 * rows

    def widen(step, carry):
        at = pl.ds(pl.multiple_of(step * step_rows, step_rows), step_rows)
        wide[at, :] = in_ref[at, :].astype(jnp.float32)
        return carry

    lax.fori_loop(0, devices // 16, widen, 0)
    for row in range(back):
        query, key, value = (
            wide[pl.ds(which * back + row, devices, stride=rows), :].astype(jnp.bfloat16)
            for which in range(3)
        )
        result[pl.ds(row, devices, stride=back), :] = attend(query, key, value, None)
    step_back = 16 * back

    def narrow(step, carry):
        at = pl.ds(pl.multiple_of(step * step_back, step_back), step_back)
        out_ref[at, :] = result[at, :].astype(jnp.bfloat16)
        return carry

    lax.fori_loop(0, devices // 16, narrow, 0)


def spatial_kernel(count, length_ref, kind_ref, q_ref, k_ref, v_ref, out_ref, list_ref):
    list_heads(kind_ref, list_ref, 1)
    positions = q_ref.shape[0]
    live = lax.broadcasted_iota(jnp.int32, (positions, positions), 1) < length_ref[0]

    def step(place, carry):
        columns = head_columns(list_ref, place)
        out_ref[:, columns] = attend(
            q_ref[:, columns], k_ref[:, columns], v_ref[:, columns], live
        ).astype(jnp.bfloat16)
        return carry

    lax.fori_loop(0, count, step, 0)


def merge_kernel(
    count, devices, kind_ref, in_ref, kept_ref, out_ref, list_ref, wide, held, sems
):
    del kept_ref
    list_heads(kind_ref, list_ref, 0)
    back = 2 * count
    step_back = 16 * back

    def widen(step, carry):
        at = pl.ds(pl.multiple_of(step * step_back, step_back), step_back)
        wide[at, :] = in_ref[at, :].astype(jnp.float32)
        return carry

    lax.fori_loop(0, devices // 16, widen, 0)

    def store(place):
        return pltpu.make_async_copy(
            held.at[place], out_ref.at[:, head_columns(list_ref, place)], sems.at[place]
        )

    for place in range(count):
        for half in range(2):
            held[place, half * devices : (half + 1) * devices, :] = wide[
                pl.ds(2 * place + half, devices, stride=back), :
            ].astype(jnp.bfloat16)
        store(place).start()
    for place in range(count):
        store(place).wait()


def params():
    return pltpu.CompilerParams(vmem_limit_bytes=VMEM_LIMIT)


def with_temporal(count, devices, queries, keys, values, lengths, kinds):
    positions, width = queries.shape
    rows, back = 6 * count, 2 * count
    smem = pl.BlockSpec(memory_space=pltpu.SMEM)
    vmem = pl.BlockSpec(memory_space=pltpu.VMEM)
    anywhere = pl.BlockSpec(memory_space=pl.ANY)
    head_list = pltpu.SMEM((HEADS + 1,), jnp.int32)

    packed = pl.pallas_call(
        functools.partial(pack_kernel, count, devices),
        out_shape=jax.ShapeDtypeStruct((devices * rows, HEAD_DIM), jnp.bfloat16),
        in_specs=[smem, anywhere, anywhere, anywhere],
        out_specs=vmem,
        scratch_shapes=[
            head_list,
            pltpu.VMEM((3 * count, positions, HEAD_DIM), jnp.bfloat16),
            pltpu.VMEM((devices * rows, HEAD_DIM), jnp.float32),
            pltpu.SemaphoreType.DMA((3 * count,)),
        ],
        compiler_params=params(),
    )(kinds, queries, keys, values)
    moved = lax.all_to_all(
        packed.reshape(devices, rows // 2, 2, HEAD_DIM), AXES, 0, 0, tiled=True
    ).reshape(devices * rows, HEAD_DIM)

    spatial_count = HEADS - count
    spatial = pl.pallas_call(
        functools.partial(spatial_kernel, spatial_count),
        out_shape=jax.ShapeDtypeStruct((positions, width), jnp.bfloat16),
        in_specs=[smem, smem, vmem, vmem, vmem],
        out_specs=vmem,
        scratch_shapes=[head_list],
        compiler_params=params(),
        cost_estimate=pl.CostEstimate(
            flops=4 * spatial_count * positions * positions * HEAD_DIM,
            bytes_accessed=8 * positions * width,
            transcendentals=spatial_count * positions * positions,
        ),
    )(lengths, kinds, queries, keys, values)

    temporal = pl.pallas_call(
        functools.partial(temporal_kernel, count, devices),
        out_shape=jax.ShapeDtypeStruct((devices * back, HEAD_DIM), jnp.bfloat16),
        in_specs=[vmem],
        out_specs=vmem,
        scratch_shapes=[
            pltpu.VMEM((devices * rows, HEAD_DIM), jnp.float32),
            pltpu.VMEM((devices * back, HEAD_DIM), jnp.float32),
        ],
        compiler_params=params(),
    )(moved)
    returned = lax.all_to_all(
        temporal.reshape(devices, back // 2, 2, HEAD_DIM), AXES, 0, 0, tiled=True
    ).reshape(devices * back, HEAD_DIM)

    return pl.pallas_call(
        functools.partial(merge_kernel, count, devices),
        out_shape=jax.ShapeDtypeStruct((positions, width), jnp.bfloat16),
        in_specs=[smem, vmem, anywhere],
        out_specs=anywhere,
        scratch_shapes=[
            head_list,
            pltpu.VMEM((devices * back, HEAD_DIM), jnp.float32),
            pltpu.VMEM((count, positions, HEAD_DIM), jnp.bfloat16),
            pltpu.SemaphoreType.DMA((count,)),
        ],
        input_output_aliases={2: 0},
        compiler_params=params(),
    )(kinds, returned, spatial)


def on_device(devices, queries, keys, values, lengths, kinds):
    branches = [
        functools.partial(with_temporal, count, devices) for count in range(1, HEADS)
    ]
    temporal_count = HEADS - jnp.sum(kinds)
    attended = lax.switch(
        temporal_count - 1, branches, queries[0], keys[0], values[0], lengths, kinds
    )
    return attended[None]


def solution(mesh):
    frames = P(AXES, None, None)
    return jax.shard_map(
        functools.partial(on_device, mesh.size),
        mesh=mesh,
        in_specs=(frames, frames, frames, P(AXES), P()),
        out_specs=frames,
        check_vma=False,
    )
```

```python
import functools
import math

import jax
import jax.numpy as jnp
from jax import lax
from jax.experimental import pallas as pl
from jax.experimental.pallas import tpu as pltpu
from jax.sharding import PartitionSpec as P

HEADS = 20
HEAD_DIM = 128
LOG2_SCALE = HEAD_DIM**-0.5 * math.log2(math.e)
AXES = ("fa", "fb")
GROUP = 4
SPATIAL_GROUP = 2
ROOMS = tuple(range(1, 20, 2))
VMEM_LIMIT = 20 * 1024 * 1024


def list_heads(kind_ref, list_ref, wanted):
    def step(head, count):
        list_ref[count] = head
        return count + (kind_ref[head] == wanted).astype(jnp.int32)

    return lax.fori_loop(0, HEADS, step, jnp.int32(0))


def each_group(count, size, work):
    def step(group, carry):
        work([jnp.minimum(group * size + i, count - 1) for i in range(size)])
        return carry

    lax.fori_loop(0, (count + size - 1) // size, step, 0)


def convert(from_ref, to_ref, rows):
    def step(block, carry):
        at = pl.ds(pl.multiple_of(block * rows, rows), rows)
        to_ref[at, :] = from_ref[at, :].astype(to_ref.dtype)
        return carry

    lax.fori_loop(0, from_ref.shape[0] // rows, step, 0)


def head_columns(list_ref, place):
    return pl.ds(pl.multiple_of(list_ref[place] * HEAD_DIM, HEAD_DIM), HEAD_DIM)


def pack_kernel(room, devices, kind_ref, q_ref, k_ref, v_ref, out_ref, list_ref, held, wide, sems):
    count = list_heads(kind_ref, list_ref, 0)
    rows = 6 * room

    def fetches(place):
        columns = head_columns(list_ref, place)
        return [
            pltpu.make_async_copy(
                ref.at[:, columns], held.at[which * room + place], sems.at[which * room + place]
            )
            for which, ref in enumerate((q_ref, k_ref, v_ref))
        ]

    def start(place, carry):
        for copy in fetches(place):
            copy.start()
        return carry

    def spread(place, carry):
        for copy in fetches(place):
            copy.wait()
        for which in range(3):
            slot = which * room + place
            for half in range(2):
                wide[pl.ds(2 * slot + half, devices, stride=rows), :] = held[
                    slot, half * devices : (half + 1) * devices, :
                ].astype(jnp.float32)
        return carry

    lax.fori_loop(0, count, start, 0)
    lax.fori_loop(0, count, spread, 0)
    convert(wide, out_ref, 8 * rows)


def attend(queries, keys, values, bias):
    scores = [
        lax.dot_general(q, k, (((1,), (1,)), ((), ())), preferred_element_type=jnp.float32)
        for q, k in zip(queries, keys, strict=True)
    ]
    if bias is not None:
        scores = [s + bias for s in scores]
    highest = [jnp.max(s, axis=-1, keepdims=True) for s in scores]
    weights = [
        jnp.exp2((s - m) * LOG2_SCALE) for s, m in zip(scores, highest, strict=True)
    ]
    totals = [jnp.sum(w, axis=-1, keepdims=True) for w in weights]
    numers = [
        jnp.dot(w.astype(jnp.bfloat16), v, preferred_element_type=jnp.float32)
        for w, v in zip(weights, values, strict=True)
    ]
    return [n / t for n, t in zip(numers, totals, strict=True)]


def temporal_kernel(room, devices, kind_ref, in_ref, out_ref, list_ref, wide, result):
    count = list_heads(kind_ref, list_ref, 0)
    rows, back = 6 * room, 2 * room
    convert(in_ref, wide, 8 * rows)

    def work(places):
        chosen = [2 * place + half for place in places for half in range(2)]
        results = attend(
            *(
                [
                    wide[pl.ds(which * back + row, devices, stride=rows), :].astype(jnp.bfloat16)
                    for row in chosen
                ]
                for which in range(3)
            ),
            None,
        )
        for row, attended in zip(chosen, results, strict=True):
            result[pl.ds(row, devices, stride=back), :] = attended

    each_group(count, GROUP, work)
    convert(result, out_ref, 8 * back)


def spatial_kernel(length_ref, kind_ref, q_ref, k_ref, v_ref, out_ref, list_ref):
    count = list_heads(kind_ref, list_ref, 1)
    positions = q_ref.shape[0]
    dead = lax.broadcasted_iota(jnp.int32, (1, positions), 1) >= length_ref[0]
    bias = jnp.where(dead, -1e30, 0.0)

    def work(places):
        columns = [head_columns(list_ref, place) for place in places]
        results = attend(*([ref[:, c] for c in columns] for ref in (q_ref, k_ref, v_ref)), bias)
        for c, attended in zip(columns, results, strict=True):
            out_ref[:, c] = attended.astype(jnp.bfloat16)

    each_group(count, SPATIAL_GROUP, work)


def merge_kernel(room, devices, kind_ref, in_ref, kept_ref, out_ref, list_ref, wide, held, sems):
    del kept_ref
    count = list_heads(kind_ref, list_ref, 0)
    back = 2 * room
    convert(in_ref, wide, 8 * back)

    def store(place):
        return pltpu.make_async_copy(
            held.at[place], out_ref.at[:, head_columns(list_ref, place)], sems.at[place]
        )

    def narrow(place, carry):
        for half in range(2):
            held[place, half * devices : (half + 1) * devices, :] = wide[
                pl.ds(2 * place + half, devices, stride=back), :
            ].astype(jnp.bfloat16)
        store(place).start()
        return carry

    def finish(place, carry):
        store(place).wait()
        return carry

    lax.fori_loop(0, count, narrow, 0)
    lax.fori_loop(0, count, finish, 0)


def params():
    return pltpu.CompilerParams(vmem_limit_bytes=VMEM_LIMIT)


def with_temporal(room, devices, queries, keys, values, lengths, kinds):
    positions, width = queries.shape
    rows, back = 6 * room, 2 * room
    smem = pl.BlockSpec(memory_space=pltpu.SMEM)
    vmem = pl.BlockSpec(memory_space=pltpu.VMEM)
    anywhere = pl.BlockSpec(memory_space=pl.ANY)
    head_list = pltpu.SMEM((HEADS + 1,), jnp.int32)

    packed = pl.pallas_call(
        functools.partial(pack_kernel, room, devices),
        out_shape=jax.ShapeDtypeStruct((devices * rows, HEAD_DIM), jnp.bfloat16),
        in_specs=[smem, anywhere, anywhere, anywhere],
        out_specs=vmem,
        scratch_shapes=[
            head_list,
            pltpu.VMEM((3 * room, positions, HEAD_DIM), jnp.bfloat16),
            pltpu.VMEM((devices * rows, HEAD_DIM), jnp.float32),
            pltpu.SemaphoreType.DMA((3 * room,)),
        ],
        compiler_params=params(),
    )(kinds, queries, keys, values)
    moved = lax.all_to_all(
        packed.reshape(devices, rows // 2, 2, HEAD_DIM), AXES, 0, 0, tiled=True
    ).reshape(devices * rows, HEAD_DIM)

    spatial_count = HEADS - room
    spatial = pl.pallas_call(
        spatial_kernel,
        out_shape=jax.ShapeDtypeStruct((positions, width), jnp.bfloat16),
        in_specs=[smem, smem, vmem, vmem, vmem],
        out_specs=vmem,
        scratch_shapes=[head_list],
        compiler_params=params(),
        cost_estimate=pl.CostEstimate(
            flops=4 * spatial_count * positions * positions * HEAD_DIM,
            bytes_accessed=8 * positions * width,
            transcendentals=spatial_count * positions * positions,
        ),
    )(lengths, kinds, queries, keys, values)

    temporal = pl.pallas_call(
        functools.partial(temporal_kernel, room, devices),
        out_shape=jax.ShapeDtypeStruct((devices * back, HEAD_DIM), jnp.bfloat16),
        in_specs=[smem, vmem],
        out_specs=vmem,
        scratch_shapes=[
            head_list,
            pltpu.VMEM((devices * rows, HEAD_DIM), jnp.float32),
            pltpu.VMEM((devices * back, HEAD_DIM), jnp.float32),
        ],
        compiler_params=params(),
    )(kinds, moved)
    returned = lax.all_to_all(
        temporal.reshape(devices, back // 2, 2, HEAD_DIM), AXES, 0, 0, tiled=True
    ).reshape(devices * back, HEAD_DIM)

    return pl.pallas_call(
        functools.partial(merge_kernel, room, devices),
        out_shape=jax.ShapeDtypeStruct((positions, width), jnp.bfloat16),
        in_specs=[smem, vmem, anywhere],
        out_specs=anywhere,
        scratch_shapes=[
            head_list,
            pltpu.VMEM((devices * back, HEAD_DIM), jnp.float32),
            pltpu.VMEM((room, positions, HEAD_DIM), jnp.bfloat16),
            pltpu.SemaphoreType.DMA((room,)),
        ],
        input_output_aliases={2: 0},
        compiler_params=params(),
    )(kinds, returned, spatial)


def on_device(devices, queries, keys, values, lengths, kinds):
    branches = [functools.partial(with_temporal, room, devices) for room in ROOMS]
    temporal_count = HEADS - jnp.sum(kinds)
    branch = sum((temporal_count > room).astype(jnp.int32) for room in ROOMS[:-1])
    attended = lax.switch(branch, branches, queries[0], keys[0], values[0], lengths, kinds)
    return attended[None]


def solution(mesh):
    frames = P(AXES, None, None)
    return jax.shard_map(
        functools.partial(on_device, mesh.size),
        mesh=mesh,
        in_specs=(frames, frames, frames, P(AXES), P()),
        out_specs=frames,
        check_vma=False,
    )
```

```python
import functools
import math

import jax
import jax.numpy as jnp
from jax import lax
from jax.experimental import pallas as pl
from jax.experimental.pallas import tpu as pltpu
from jax.sharding import PartitionSpec as P

HEADS = 20
HEAD_DIM = 128
LOG2_SCALE = HEAD_DIM**-0.5 * math.log2(math.e)
AXES = ("fa", "fb")
GROUP = 10
SPATIAL_GROUP = 4
ROOMS = tuple(range(1, 20, 2))
VMEM_LIMIT = 20 * 1024 * 1024


def list_heads(kind_ref, list_ref, wanted):
    def step(head, count):
        list_ref[count] = head
        return count + (kind_ref[head] == wanted).astype(jnp.int32)

    return lax.fori_loop(0, HEADS, step, jnp.int32(0))


def each_group(count, size, work):
    def step(group, carry):
        work([jnp.minimum(group * size + i, count - 1) for i in range(size)])
        return carry

    lax.fori_loop(0, (count + size - 1) // size, step, 0)


def convert(from_ref, to_ref, rows):
    def step(block, carry):
        at = pl.ds(pl.multiple_of(block * rows, rows), rows)
        to_ref[at, :] = from_ref[at, :].astype(to_ref.dtype)
        return carry

    lax.fori_loop(0, from_ref.shape[0] // rows, step, 0)


def head_columns(list_ref, place):
    return pl.ds(pl.multiple_of(list_ref[place] * HEAD_DIM, HEAD_DIM), HEAD_DIM)


def pack_kernel(room, devices, kind_ref, q_ref, k_ref, v_ref, out_ref, list_ref, held, wide, sems):
    count = list_heads(kind_ref, list_ref, 0)
    rows = 6 * room

    def fetches(place):
        columns = head_columns(list_ref, place)
        return [
            pltpu.make_async_copy(
                ref.at[:, columns], held.at[which * room + place], sems.at[which * room + place]
            )
            for which, ref in enumerate((q_ref, k_ref, v_ref))
        ]

    def start(place, carry):
        for copy in fetches(place):
            copy.start()
        return carry

    def spread(place, carry):
        for copy in fetches(place):
            copy.wait()
        for which in range(3):
            slot = which * room + place
            for half in range(2):
                wide[pl.ds(2 * slot + half, devices, stride=rows), :] = held[
                    slot, half * devices : (half + 1) * devices, :
                ].astype(jnp.float32)
        return carry

    lax.fori_loop(0, count, start, 0)
    lax.fori_loop(0, count, spread, 0)
    convert(wide, out_ref, 8 * rows)


def attend(queries, keys, values, bias):
    scores = [
        lax.dot_general(q, k, (((1,), (1,)), ((), ())), preferred_element_type=jnp.float32)
        for q, k in zip(queries, keys, strict=True)
    ]
    if bias is not None:
        scores = [s + bias for s in scores]
    highest = [jnp.max(s, axis=-1, keepdims=True) for s in scores]
    weights = [
        jnp.exp2((s - m) * LOG2_SCALE) for s, m in zip(scores, highest, strict=True)
    ]
    totals = [jnp.sum(w, axis=-1, keepdims=True) for w in weights]
    numers = [
        jnp.dot(w.astype(jnp.bfloat16), v, preferred_element_type=jnp.float32)
        for w, v in zip(weights, values, strict=True)
    ]
    return [n / t for n, t in zip(numers, totals, strict=True)]


def temporal_kernel(room, devices, in_ref, out_ref, wide, result):
    rows, back = 6 * room, 2 * room
    convert(in_ref, wide, 8 * rows)

    def work(places):
        chosen = [2 * place + half for place in places for half in range(2)]
        results = attend(
            *(
                [
                    wide[pl.ds(which * back + row, devices, stride=rows), :].astype(jnp.bfloat16)
                    for row in chosen
                ]
                for which in range(3)
            ),
            None,
        )
        for row, attended in zip(chosen, results, strict=True):
            result[pl.ds(row, devices, stride=back), :] = attended

    each_group(room, -(-room // -(-room // GROUP)), work)
    convert(result, out_ref, 8 * back)


def spatial_kernel(length_ref, kind_ref, q_ref, k_ref, v_ref, out_ref, list_ref):
    count = list_heads(kind_ref, list_ref, 1)
    positions = q_ref.shape[0]
    dead = lax.broadcasted_iota(jnp.int32, (1, positions), 1) >= length_ref[0]
    bias = jnp.where(dead, -1e30, 0.0)

    def work(places):
        columns = [head_columns(list_ref, place) for place in places]
        results = attend(*([ref[:, c] for c in columns] for ref in (q_ref, k_ref, v_ref)), bias)
        for c, attended in zip(columns, results, strict=True):
            out_ref[:, c] = attended.astype(jnp.bfloat16)

    each_group(count, SPATIAL_GROUP, work)


def merge_kernel(
    room, devices, kind_ref, in_ref, kept_ref, out_ref, kinds, list_ref, wide, held, kind_sem, sems
):
    del kept_ref
    back = 2 * room
    fetch = pltpu.make_async_copy(kind_ref, kinds, kind_sem)
    fetch.start()
    convert(in_ref, wide, 8 * back)
    fetch.wait()
    count = list_heads(kinds, list_ref, 0)

    def store(place):
        return pltpu.make_async_copy(
            held.at[place], out_ref.at[:, head_columns(list_ref, place)], sems.at[place]
        )

    def narrow(place, carry):
        for half in range(2):
            held[place, half * devices : (half + 1) * devices, :] = wide[
                pl.ds(2 * place + half, devices, stride=back), :
            ].astype(jnp.bfloat16)
        store(place).start()
        return carry

    def finish(place, carry):
        store(place).wait()
        return carry

    lax.fori_loop(0, count, narrow, 0)
    lax.fori_loop(0, count, finish, 0)


def params():
    return pltpu.CompilerParams(vmem_limit_bytes=VMEM_LIMIT)


def with_temporal(room, devices, queries, keys, values, lengths, kinds):
    positions, width = queries.shape
    rows, back = 6 * room, 2 * room
    smem = pl.BlockSpec(memory_space=pltpu.SMEM)
    vmem = pl.BlockSpec(memory_space=pltpu.VMEM)
    anywhere = pl.BlockSpec(memory_space=pl.ANY)
    head_list = pltpu.SMEM((HEADS + 1,), jnp.int32)

    packed = pl.pallas_call(
        functools.partial(pack_kernel, room, devices),
        out_shape=jax.ShapeDtypeStruct((devices * rows, HEAD_DIM), jnp.bfloat16),
        in_specs=[smem, anywhere, anywhere, anywhere],
        out_specs=vmem,
        scratch_shapes=[
            head_list,
            pltpu.VMEM((3 * room, positions, HEAD_DIM), jnp.bfloat16),
            pltpu.VMEM((devices * rows, HEAD_DIM), jnp.float32),
            pltpu.SemaphoreType.DMA((3 * room,)),
        ],
        compiler_params=params(),
    )(kinds, queries, keys, values)
    moved = lax.all_to_all(
        packed.reshape(devices, rows // 2, 2, HEAD_DIM), AXES, 0, 0, tiled=True
    ).reshape(devices * rows, HEAD_DIM)

    spatial_count = HEADS - room
    spatial = pl.pallas_call(
        spatial_kernel,
        out_shape=jax.ShapeDtypeStruct((positions, width), jnp.bfloat16),
        in_specs=[smem, smem, vmem, vmem, vmem],
        out_specs=vmem,
        scratch_shapes=[head_list],
        compiler_params=params(),
        cost_estimate=pl.CostEstimate(
            flops=4 * spatial_count * positions * positions * HEAD_DIM,
            bytes_accessed=8 * positions * width,
            transcendentals=spatial_count * positions * positions,
        ),
    )(lengths, kinds, queries, keys, values)

    temporal = pl.pallas_call(
        functools.partial(temporal_kernel, room, devices),
        out_shape=jax.ShapeDtypeStruct((devices * back, HEAD_DIM), jnp.bfloat16),
        in_specs=[vmem],
        out_specs=vmem,
        scratch_shapes=[
            pltpu.VMEM((devices * rows, HEAD_DIM), jnp.float32),
            pltpu.VMEM((devices * back, HEAD_DIM), jnp.float32),
        ],
        compiler_params=params(),
    )(moved)
    returned = lax.all_to_all(
        temporal.reshape(devices, back // 2, 2, HEAD_DIM), AXES, 0, 0, tiled=True
    ).reshape(devices * back, HEAD_DIM)

    return pl.pallas_call(
        functools.partial(merge_kernel, room, devices),
        out_shape=jax.ShapeDtypeStruct((positions, width), jnp.bfloat16),
        in_specs=[anywhere, vmem, anywhere],
        out_specs=anywhere,
        scratch_shapes=[
            pltpu.SMEM((HEADS,), jnp.int32),
            head_list,
            pltpu.VMEM((devices * back, HEAD_DIM), jnp.float32),
            pltpu.VMEM((room, positions, HEAD_DIM), jnp.bfloat16),
            pltpu.SemaphoreType.DMA(()),
            pltpu.SemaphoreType.DMA((room,)),
        ],
        input_output_aliases={2: 0},
        compiler_params=params(),
    )(kinds, returned, spatial)


def on_device(devices, queries, keys, values, lengths, kinds):
    branches = [functools.partial(with_temporal, room, devices) for room in ROOMS]
    temporal_count = HEADS - jnp.sum(kinds)
    branch = sum((temporal_count > room).astype(jnp.int32) for room in ROOMS[:-1])
    attended = lax.switch(branch, branches, queries[0], keys[0], values[0], lengths, kinds)
    return attended[None]


def solution(mesh):
    frames = P(AXES, None, None)
    return jax.shard_map(
        functools.partial(on_device, mesh.size),
        mesh=mesh,
        in_specs=(frames, frames, frames, P(AXES), P()),
        out_specs=frames,
        check_vma=False,
    )
```

```python
import functools
import math

import jax
import jax.numpy as jnp
from jax import lax
from jax.experimental import pallas as pl
from jax.experimental.pallas import tpu as pltpu
from jax.sharding import PartitionSpec as P

HEADS = 20
HEAD_DIM = 128
LOG2_SCALE = HEAD_DIM**-0.5 * math.log2(math.e)
AXES = ("fa", "fb")
GROUP = 7
SPATIAL_GROUP = 2
ROOMS = tuple(range(1, 20, 2))
VMEM_LIMIT = 20 * 1024 * 1024


def list_heads(kind_ref, list_ref, wanted):
    def step(head, count):
        list_ref[count] = head
        return count + (kind_ref[head] == wanted).astype(jnp.int32)

    return lax.fori_loop(0, HEADS, step, jnp.int32(0))


def list_heads_of(kinds, list_ref, wanted):
    count = jnp.int32(0)
    for head in range(HEADS):
        list_ref[count] = head
        count = count + (kinds[0, head] == wanted).astype(jnp.int32)
    return count


def each_group(count, size, work):
    if isinstance(count, int) and count <= size:
        work(range(count))
        return

    def step(group, carry):
        work([jnp.minimum(group * size + i, count - 1) for i in range(size)])
        return carry

    lax.fori_loop(0, (count + size - 1) // size, step, 0)


def convert(from_ref, to_ref, rows):
    def step(block, carry):
        at = pl.ds(pl.multiple_of(block * rows, rows), rows)
        to_ref[at, :] = from_ref[at, :].astype(to_ref.dtype)
        return carry

    lax.fori_loop(0, min(from_ref.shape[0], to_ref.shape[0]) // rows, step, 0)


def head_columns(list_ref, place):
    return pl.ds(pl.multiple_of(list_ref[place] * HEAD_DIM, HEAD_DIM), HEAD_DIM)


def pack_kernel(room, devices, kind_ref, q_ref, k_ref, v_ref, out_ref, list_ref, held, wide, sems):
    count = list_heads(kind_ref, list_ref, 0)
    rows = 6 * room

    def fetches(place):
        columns = head_columns(list_ref, place)
        return [
            pltpu.make_async_copy(
                ref.at[:, columns], held.at[which * room + place], sems.at[which * room + place]
            )
            for which, ref in enumerate((q_ref, k_ref, v_ref))
        ]

    def start(place, carry):
        for copy in fetches(place):
            copy.start()
        return carry

    def spread(place, carry):
        for copy in fetches(place):
            copy.wait()
        for which in range(3):
            slot = which * room + place
            for half in range(2):
                wide[pl.ds(2 * slot + half, devices, stride=rows), :] = held[
                    slot, half * devices : (half + 1) * devices, :
                ].astype(jnp.float32)
        return carry

    lax.fori_loop(0, count, start, 0)
    lax.fori_loop(0, count, spread, 0)
    convert(wide, out_ref, 8 * rows)


def attend(queries, keys, values, bias):
    scores = [
        lax.dot_general(q, k, (((1,), (1,)), ((), ())), preferred_element_type=jnp.float32)
        for q, k in zip(queries, keys, strict=True)
    ]
    if bias is not None:
        scores = [s + bias for s in scores]
    highest = [jnp.max(s, axis=-1, keepdims=True) for s in scores]
    weights = [
        jnp.exp2((s - m) * LOG2_SCALE) for s, m in zip(scores, highest, strict=True)
    ]
    totals = [jnp.sum(w, axis=-1, keepdims=True) for w in weights]
    numers = [
        jnp.dot(w.astype(jnp.bfloat16), v, preferred_element_type=jnp.float32)
        for w, v in zip(weights, values, strict=True)
    ]
    return [n / t for n, t in zip(numers, totals, strict=True)]


def temporal_kernel(room, devices, in_ref, out_ref, wide, result):
    rows, back = 6 * room, 2 * room
    convert(in_ref, wide, 8 * rows)

    def work(places):
        chosen = [2 * place + half for place in places for half in range(2)]
        results = attend(
            *(
                [
                    wide[pl.ds(which * back + row, devices, stride=rows), :].astype(jnp.bfloat16)
                    for row in chosen
                ]
                for which in range(3)
            ),
            None,
        )
        for row, attended in zip(chosen, results, strict=True):
            result[pl.ds(row, devices, stride=back), :] = attended

    each_group(room, -(-room // -(-room // GROUP)), work)
    convert(result, out_ref, 8 * back)


def spatial_kernel(length_ref, kind_ref, q_ref, k_ref, v_ref, out_ref, list_ref):
    count = list_heads_of(kind_ref[...], list_ref, 1)
    positions = q_ref.shape[0]
    dead = lax.broadcasted_iota(jnp.int32, (1, positions), 1) >= length_ref[...]
    bias = jnp.where(dead, -1e30, 0.0)

    def work(places):
        columns = [head_columns(list_ref, place) for place in places]
        results = attend(*([ref[:, c] for c in columns] for ref in (q_ref, k_ref, v_ref)), bias)
        for c, attended in zip(columns, results, strict=True):
            out_ref[:, c] = attended.astype(jnp.bfloat16)

    each_group(count, SPATIAL_GROUP, work)


def merge_kernel(room, devices, kind_ref, in_ref, kept_ref, out_ref, list_ref, wide, held, sems):
    del kept_ref
    back = 2 * room
    count = list_heads_of(kind_ref[...], list_ref, 0)
    convert(in_ref, wide, 8 * back)

    def store(place):
        return pltpu.make_async_copy(
            held.at[place], out_ref.at[:, head_columns(list_ref, place)], sems.at[place]
        )

    def narrow(place, carry):
        for half in range(2):
            held[place, half * devices : (half + 1) * devices, :] = wide[
                pl.ds(2 * place + half, devices, stride=back), :
            ].astype(jnp.bfloat16)
        store(place).start()
        return carry

    def finish(place, carry):
        store(place).wait()
        return carry

    lax.fori_loop(0, count, narrow, 0)
    lax.fori_loop(0, count, finish, 0)


def params():
    return pltpu.CompilerParams(vmem_limit_bytes=VMEM_LIMIT)


def with_temporal(room, devices, queries, keys, values, lengths, kinds):
    positions, width = queries.shape
    rows, back = 6 * room, 2 * room
    smem = pl.BlockSpec(memory_space=pltpu.SMEM)
    vmem = pl.BlockSpec(memory_space=pltpu.VMEM)
    anywhere = pl.BlockSpec(memory_space=pl.ANY)
    head_list = pltpu.SMEM((HEADS + 1,), jnp.int32)

    packed = pl.pallas_call(
        functools.partial(pack_kernel, room, devices),
        out_shape=jax.ShapeDtypeStruct((devices * rows, HEAD_DIM), jnp.bfloat16),
        in_specs=[smem, anywhere, anywhere, anywhere],
        out_specs=vmem,
        scratch_shapes=[
            head_list,
            pltpu.VMEM((3 * room, positions, HEAD_DIM), jnp.bfloat16),
            pltpu.VMEM(((devices + 1) * rows, HEAD_DIM), jnp.float32),
            pltpu.SemaphoreType.DMA((3 * room,)),
        ],
        compiler_params=params(),
    )(kinds, queries, keys, values)
    moved = lax.all_to_all(
        packed.reshape(devices, rows // 2, 2, HEAD_DIM), AXES, 0, 0, tiled=True
    ).reshape(devices * rows, HEAD_DIM)

    spatial_count = HEADS - room
    spatial = pl.pallas_call(
        spatial_kernel,
        out_shape=jax.ShapeDtypeStruct((positions, width), jnp.bfloat16),
        in_specs=[vmem] * 5,
        out_specs=vmem,
        scratch_shapes=[head_list],
        compiler_params=params(),
        cost_estimate=pl.CostEstimate(
            flops=4 * spatial_count * positions * positions * HEAD_DIM,
            bytes_accessed=8 * positions * width,
            transcendentals=spatial_count * positions * positions,
        ),
    )(lengths.reshape(1, 1), kinds.reshape(1, HEADS), queries, keys, values)

    temporal = pl.pallas_call(
        functools.partial(temporal_kernel, room, devices),
        out_shape=jax.ShapeDtypeStruct((devices * back, HEAD_DIM), jnp.bfloat16),
        in_specs=[vmem],
        out_specs=vmem,
        scratch_shapes=[
            pltpu.VMEM(((devices + 1) * rows, HEAD_DIM), jnp.float32),
            pltpu.VMEM(((devices + 1) * back, HEAD_DIM), jnp.float32),
        ],
        compiler_params=params(),
    )(moved)
    returned = lax.all_to_all(
        temporal.reshape(devices, back // 2, 2, HEAD_DIM), AXES, 0, 0, tiled=True
    ).reshape(devices * back, HEAD_DIM)

    return pl.pallas_call(
        functools.partial(merge_kernel, room, devices),
        out_shape=jax.ShapeDtypeStruct((positions, width), jnp.bfloat16),
        in_specs=[vmem, vmem, anywhere],
        out_specs=anywhere,
        scratch_shapes=[
            head_list,
            pltpu.VMEM(((devices + 1) * back, HEAD_DIM), jnp.float32),
            pltpu.VMEM((room, positions, HEAD_DIM), jnp.bfloat16),
            pltpu.SemaphoreType.DMA((room,)),
        ],
        input_output_aliases={2: 0},
        compiler_params=params(),
    )(kinds.reshape(1, HEADS), returned, spatial)


def on_device(devices, queries, keys, values, lengths, kinds):
    branches = [functools.partial(with_temporal, room, devices) for room in ROOMS]
    temporal_count = HEADS - jnp.sum(kinds)
    branch = sum((temporal_count > room).astype(jnp.int32) for room in ROOMS[:-1])
    attended = lax.switch(branch, branches, queries[0], keys[0], values[0], lengths, kinds)
    return attended[None]


def solution(mesh):
    frames = P(AXES, None, None)
    return jax.shard_map(
        functools.partial(on_device, mesh.size),
        mesh=mesh,
        in_specs=(frames, frames, frames, P(AXES), P()),
        out_specs=frames,
        check_vma=False,
    )
```

```python
import functools
import math

import jax
import jax.numpy as jnp
from jax import lax
from jax.experimental import pallas as pl
from jax.experimental.pallas import tpu as pltpu
from jax.sharding import PartitionSpec as P

HEADS = 20
HEAD_DIM = 128
LOG2_SCALE = HEAD_DIM**-0.5 * math.log2(math.e)
AXES = ("fa", "fb")
GROUP = 7
SPATIAL_GROUP = 2
ROOMS = tuple(range(1, 20, 2))
VMEM_LIMIT = 20 * 1024 * 1024


def list_heads(kind_ref, list_ref, wanted):
    def step(head, count):
        list_ref[count] = head
        return count + (kind_ref[head] == wanted).astype(jnp.int32)

    return lax.fori_loop(0, HEADS, step, jnp.int32(0))


def list_heads_of(kinds, list_ref, wanted):
    count = jnp.int32(0)
    for head in range(HEADS):
        list_ref[count] = head
        count = count + (kinds[0, head] == wanted).astype(jnp.int32)
    return count


def each_group(count, size, work):
    if isinstance(count, int) and count <= size:
        work(range(count))
        return

    def step(group, carry):
        work([jnp.minimum(group * size + i, count - 1) for i in range(size)])
        return carry

    lax.fori_loop(0, (count + size - 1) // size, step, 0)


def convert(from_ref, to_ref, rows):
    def step(block, carry):
        at = pl.ds(pl.multiple_of(block * rows, rows), rows)
        to_ref[at, :] = from_ref[at, :].astype(to_ref.dtype)
        return carry

    lax.fori_loop(0, min(from_ref.shape[0], to_ref.shape[0]) // rows, step, 0)


def head_columns(list_ref, place):
    return pl.ds(pl.multiple_of(list_ref[place] * HEAD_DIM, HEAD_DIM), HEAD_DIM)


def pack_kernel(room, devices, kind_ref, q_ref, k_ref, v_ref, out_ref, list_ref, held, wide, sems):
    rows = 6 * room

    def fetches(place):
        columns = head_columns(list_ref, place)
        return [
            pltpu.make_async_copy(
                ref.at[:, columns], held.at[which * room + place], sems.at[which * room + place]
            )
            for which, ref in enumerate((q_ref, k_ref, v_ref))
        ]

    def find(head, count):
        temporal = kind_ref[head] == 0

        @pl.when(temporal)
        def _():
            list_ref[count] = head
            for copy in fetches(count):
                copy.start()

        return count + temporal.astype(jnp.int32)

    def spread(place, carry):
        for copy in fetches(place):
            copy.wait()
        for which in range(3):
            slot = which * room + place
            for half in range(2):
                wide[pl.ds(2 * slot + half, devices, stride=rows), :] = held[
                    slot, half * devices : (half + 1) * devices, :
                ].astype(jnp.float32)
        return carry

    count = lax.fori_loop(0, HEADS, find, jnp.int32(0))
    lax.fori_loop(0, count, spread, 0)
    convert(wide, out_ref, 8 * rows)


def attend(queries, keys, values, bias):
    scores = [
        lax.dot_general(q, k, (((1,), (1,)), ((), ())), preferred_element_type=jnp.float32)
        for q, k in zip(queries, keys, strict=True)
    ]
    if bias is not None:
        scores = [s + bias for s in scores]
    highest = [jnp.max(s, axis=-1, keepdims=True) for s in scores]
    weights = [
        jnp.exp2((s - m) * LOG2_SCALE) for s, m in zip(scores, highest, strict=True)
    ]
    totals = [jnp.sum(w, axis=-1, keepdims=True) for w in weights]
    numers = [
        jnp.dot(w.astype(jnp.bfloat16), v, preferred_element_type=jnp.float32)
        for w, v in zip(weights, values, strict=True)
    ]
    return [n / t for n, t in zip(numers, totals, strict=True)]


def temporal_kernel(room, devices, in_ref, out_ref, wide, result):
    rows, back = 6 * room, 2 * room
    convert(in_ref, wide, 8 * rows)

    def work(places):
        chosen = [2 * place + half for place in places for half in range(2)]
        results = attend(
            *(
                [
                    wide[pl.ds(which * back + row, devices, stride=rows), :].astype(jnp.bfloat16)
                    for row in chosen
                ]
                for which in range(3)
            ),
            None,
        )
        for row, attended in zip(chosen, results, strict=True):
            result[pl.ds(row, devices, stride=back), :] = attended

    each_group(room, -(-room // -(-room // GROUP)), work)
    convert(result, out_ref, 8 * back)


def spatial_kernel(length_ref, kind_ref, q_ref, k_ref, v_ref, out_ref, list_ref):
    count = list_heads_of(kind_ref[...], list_ref, 1)
    positions = q_ref.shape[0]
    dead = lax.broadcasted_iota(jnp.int32, (1, positions), 1) >= length_ref[...]
    bias = jnp.where(dead, -1e30, 0.0)

    def work(places):
        columns = [head_columns(list_ref, place) for place in places]
        results = attend(*([ref[:, c] for c in columns] for ref in (q_ref, k_ref, v_ref)), bias)
        for c, attended in zip(columns, results, strict=True):
            out_ref[:, c] = attended.astype(jnp.bfloat16)

    each_group(count, SPATIAL_GROUP, work)


def merge_kernel(room, devices, kind_ref, in_ref, kept_ref, out_ref, list_ref, wide, held, sems):
    del kept_ref
    back = 2 * room
    count = list_heads_of(kind_ref[...], list_ref, 0)
    convert(in_ref, wide, 8 * back)

    def store(place):
        return pltpu.make_async_copy(
            held.at[place], out_ref.at[:, head_columns(list_ref, place)], sems.at[place]
        )

    def narrow(place, carry):
        for half in range(2):
            held[place, half * devices : (half + 1) * devices, :] = wide[
                pl.ds(2 * place + half, devices, stride=back), :
            ].astype(jnp.bfloat16)
        store(place).start()
        return carry

    def finish(place, carry):
        store(place).wait()
        return carry

    lax.fori_loop(0, count, narrow, 0)
    lax.fori_loop(0, count, finish, 0)


def params():
    return pltpu.CompilerParams(vmem_limit_bytes=VMEM_LIMIT)


def with_temporal(room, devices, queries, keys, values, lengths, kinds):
    positions, width = queries.shape
    rows, back = 6 * room, 2 * room
    smem = pl.BlockSpec(memory_space=pltpu.SMEM)
    vmem = pl.BlockSpec(memory_space=pltpu.VMEM)
    anywhere = pl.BlockSpec(memory_space=pl.ANY)
    head_list = pltpu.SMEM((HEADS + 1,), jnp.int32)

    packed = pl.pallas_call(
        functools.partial(pack_kernel, room, devices),
        out_shape=jax.ShapeDtypeStruct((devices * rows, HEAD_DIM), jnp.bfloat16),
        in_specs=[smem, anywhere, anywhere, anywhere],
        out_specs=vmem,
        scratch_shapes=[
            head_list,
            pltpu.VMEM((3 * room, positions, HEAD_DIM), jnp.bfloat16),
            pltpu.VMEM(((devices + 1) * rows, HEAD_DIM), jnp.float32),
            pltpu.SemaphoreType.DMA((3 * room,)),
        ],
        compiler_params=params(),
    )(kinds, queries, keys, values)
    moved = lax.all_to_all(
        packed.reshape(devices, rows // 2, 2, HEAD_DIM), AXES, 0, 0, tiled=True
    ).reshape(devices * rows, HEAD_DIM)

    spatial_count = HEADS - room
    spatial = pl.pallas_call(
        spatial_kernel,
        out_shape=jax.ShapeDtypeStruct((positions, width), jnp.bfloat16),
        in_specs=[vmem] * 5,
        out_specs=vmem,
        scratch_shapes=[head_list],
        compiler_params=params(),
        cost_estimate=pl.CostEstimate(
            flops=4 * spatial_count * positions * positions * HEAD_DIM,
            bytes_accessed=8 * positions * width,
            transcendentals=spatial_count * positions * positions,
        ),
    )(lengths.reshape(1, 1), kinds.reshape(1, HEADS), queries, keys, values)

    temporal = pl.pallas_call(
        functools.partial(temporal_kernel, room, devices),
        out_shape=jax.ShapeDtypeStruct((devices * back, HEAD_DIM), jnp.bfloat16),
        in_specs=[vmem],
        out_specs=vmem,
        scratch_shapes=[
            pltpu.VMEM(((devices + 1) * rows, HEAD_DIM), jnp.float32),
            pltpu.VMEM(((devices + 1) * back, HEAD_DIM), jnp.float32),
        ],
        compiler_params=params(),
    )(moved)
    returned = lax.all_to_all(
        temporal.reshape(devices, back // 2, 2, HEAD_DIM), AXES, 0, 0, tiled=True
    ).reshape(devices * back, HEAD_DIM)

    return pl.pallas_call(
        functools.partial(merge_kernel, room, devices),
        out_shape=jax.ShapeDtypeStruct((positions, width), jnp.bfloat16),
        in_specs=[vmem, vmem, anywhere],
        out_specs=anywhere,
        scratch_shapes=[
            head_list,
            pltpu.VMEM(((devices + 1) * back, HEAD_DIM), jnp.float32),
            pltpu.VMEM((room, positions, HEAD_DIM), jnp.bfloat16),
            pltpu.SemaphoreType.DMA((room,)),
        ],
        input_output_aliases={2: 0},
        compiler_params=params(),
    )(kinds.reshape(1, HEADS), returned, spatial)


def on_device(devices, queries, keys, values, lengths, kinds):
    branches = [functools.partial(with_temporal, room, devices) for room in ROOMS]
    temporal_count = HEADS - jnp.sum(kinds)
    branch = sum((temporal_count > room).astype(jnp.int32) for room in ROOMS[:-1])
    attended = lax.switch(branch, branches, queries[0], keys[0], values[0], lengths, kinds)
    return attended[None]


def solution(mesh):
    frames = P(AXES, None, None)
    return jax.shard_map(
        functools.partial(on_device, mesh.size),
        mesh=mesh,
        in_specs=(frames, frames, frames, P(AXES), P()),
        out_specs=frames,
        check_vma=False,
    )
```
